32 devices in a mesh: depth: 8 (over z, y), chan: 4 (over x, core).
Axes of the slice: x: 2, y: 2, z: 4, core: 2. Of those that a mesh axis runs over, the one named last changes fastest.
Arguments:
- volume: bfloat16 [256, 8, 4096], P('chan', 'depth'), may hold values from -6 to 6
- w_first: bfloat16 [27, 256, 256], P(None, 'chan'), may hold values from -0.078125 to 0.078125
- b_first: float32 [256], P('chan'), may hold values from -3 to 3
- w_second: bfloat16 [27, 256, 256], P(None, None, 'chan'), may hold values from -0.078125 to 0.078125
- b_second: float32 [256], P('chan'), may hold values from -3 to 3
Outputs:
- block_out: bfloat16 [256, 8, 4096], P('chan', 'depth')
The draws below stay inside these ranges and needn't reach their ends.
All inputs are finite; a program needn't handle non-finite values.
Results may differ from the reference program's by a relative error of at most 0.0043.
Values may be sent and summed in bfloat16 or wider, within the bound.
A program may use at most 128 MiB of HBM per device.

```python
import jax
import jax.numpy as jnp
from jax import lax

C = 256
H = 64
W = 64
D = 8
HW = 4096


def level_of(key, extent, pieces, low, top_value):
    loudness = 1.0
    for position, parts in pieces:
        draws = jax.random.uniform(jax.random.fold_in(jax.random.fold_in(key, 6), position), (parts,), jnp.float32, low / len(pieces), top_value / len(pieces))
        loudness = loudness * jnp.repeat(jnp.exp(draws), extent[position] // parts).reshape((-1,) + (1,) * (len(extent) - 1 - position))
    return loudness


def normal_values(own_key, shape, width, limit, cuts=(), held_as=jnp.bfloat16):
    level = level_of(own_key, shape, cuts, -0.22, 0.18) if cuts else 1.0
    entries = jax.random.normal(own_key, shape, jnp.float32) * width * level
    return jnp.minimum(jnp.maximum(entries, -limit), limit).astype(held_as)


def setup_inputs(seed: int = 0) -> dict:
    arg_keys = jax.random.split(jax.random.key(seed), 6)
    volume = normal_values(arg_keys[0], (C, D, HW), 1.0, 6.0, ((0, 4), (1, 8)))
    w_first = normal_values(arg_keys[1], (27, C, C), (27 * C) ** -0.5, 0.078125, ((1, 4),))
    b_first = normal_values(arg_keys[2], (C,), 0.5, 3.0, ((0, 4),), jnp.float32)
    w_second = normal_values(arg_keys[3], (27, C, C), (27 * C) ** -0.5, 0.078125, ((2, 4),))
    b_second = normal_values(arg_keys[4], (C,), 0.5, 3.0, ((0, 4),), jnp.float32)
    return {"volume": volume, "w_first": w_first, "b_first": b_first, "w_second": w_second, "b_second": b_second}


def convolve(source, filters):
    in_chan, planes, cell_count = source.shape
    out_chan = filters.shape[2]
    volume_f = source.astype(jnp.float32).reshape(1, in_chan, planes, H, W)
    kernel = filters.astype(jnp.float32).reshape(3, 3, 3, in_chan, out_chan).transpose(4, 3, 0, 1, 2)
    result = lax.conv_general_dilated(volume_f, kernel, (1, 1, 1), ((1, 1), (1, 1), (1, 1)),
                                      dimension_numbers=("NCDHW", "OIDHW", "NCDHW"),
                                      precision=lax.Precision.HIGHEST)
    return result.reshape(out_chan, planes, cell_count)


def reference(volume, w_first, b_first, w_second, b_second):
    first_sum = convolve(volume, w_first) + b_first[:, None, None]
    hidden = jnp.maximum(first_sum, 0.0).astype(jnp.bfloat16)
    second_sum = convolve(hidden, w_second) + b_second[:, None, None]
    return second_sum.astype(jnp.bfloat16)
```

```python
import functools

import jax
import jax.numpy as jnp
from jax import lax
from jax.experimental import pallas as pl
from jax.experimental.pallas import tpu as pltpu
from jax.sharding import PartitionSpec as P

W = 64
PAD = 128
CHUNKS = 4
MESH = pl.DeviceIdType.MESH


def kernel(nd, nc, vol, w1, b1, w2, b2, out,
           xlo, xmid, xhi, w1t, w2t, cols1, cols2, s1s, s1r, keep, s2s, s2r,
           hpad, ps, pr, keep2,
           hal_s, hal_r, s1_ss, s1_rs, s2_ss, s2_rs, ag_ss, ag_rs, par_s, par_r):
    chan, cells = vol.shape
    total = chan * nc
    half = nc // 2
    size = cells // CHUNKS
    d = lax.axis_index("depth")
    c = lax.axis_index("chan")
    core = lax.rem(c, 2)
    chip = c // 2
    sibling = 2 * chip + 1 - core
    has_up = d < nd - 1
    has_down = d > 0

    def peer(k):
        return 2 * lax.rem(chip + k, half) + core

    zero_edge = jnp.zeros((chan, PAD), jnp.bfloat16)
    for pad in (xlo, xmid, xhi):
        pad[:, 0:PAD] = zero_edge
        pad[:, PAD + cells:] = zero_edge
    hpad[:, 0:PAD] = jnp.zeros((total, PAD), jnp.bfloat16)
    hpad[:, PAD + cells:] = jnp.zeros((total, PAD), jnp.bfloat16)

    @pl.when(d == 0)
    def _():
        xlo[:, PAD:PAD + cells] = jnp.zeros((chan, cells), jnp.bfloat16)
        pr[0] = jnp.zeros((chan, cells), jnp.bfloat16)

    @pl.when(d == nd - 1)
    def _():
        xhi[:, PAD:PAD + cells] = jnp.zeros((chan, cells), jnp.bfloat16)
        pr[1] = jnp.zeros((chan, cells), jnp.bfloat16)

    barrier = pltpu.get_barrier_semaphore()

    @pl.when(has_up)
    def _():
        pl.semaphore_signal(barrier, inc=1, device_id={"depth": d + 1}, device_id_type=MESH)

    @pl.when(has_down)
    def _():
        pl.semaphore_signal(barrier, inc=1, device_id={"depth": d - 1}, device_id_type=MESH)

    pl.semaphore_signal(barrier, inc=1, device_id={"chan": sibling}, device_id_type=MESH)
    for k in range(1, half):
        pl.semaphore_signal(barrier, inc=1, device_id={"chan": peer(k)}, device_id_type=MESH)

    pl.semaphore_wait(barrier, half + has_up.astype(jnp.int32) + has_down.astype(jnp.int32))

    def remote(src, dst, send, recv, where):
        return pltpu.make_async_remote_copy(
            src_ref=src, dst_ref=dst, send_sem=send, recv_sem=recv,
            device_id=where, device_id_type=MESH)

    def halo_up(n):
        return remote(vol.at[:, pl.ds(n * size, size)], xlo.at[:, pl.ds(PAD + n * size, size)],
                      hal_s.at[0, n], hal_r.at[0, n], {"depth": d + 1})

    def halo_down(n):
        return remote(vol.at[:, pl.ds(n * size, size)], xhi.at[:, pl.ds(PAD + n * size, size)],
                      hal_s.at[1, n], hal_r.at[1, n], {"depth": d - 1})

    for n in range(CHUNKS):
        @pl.when(has_up)
        def _():
            halo_up(n).start()

        @pl.when(has_down)
        def _():
            halo_down(n).start()

    xmid[:, PAD:PAD + cells] = vol[...]
    taps = 27 * chan
    for begin in range(0, taps, 128):
        end = min(begin + 128, taps)
        w1t[:, begin:end] = w1[begin:end, :].T
    for kd in range(3):
        for kk in range(9):
            w2t[kd * chan:(kd + 1) * chan, kk * total:(kk + 1) * total] = w2[kd * 9 + kk].T

    column = lax.broadcasted_iota(jnp.int32, (1, size), 1) % W
    left = jnp.where(column >= 1, 1.0, 0.0).astype(jnp.bfloat16)
    right = jnp.where(column < W - 1, 1.0, 0.0).astype(jnp.bfloat16)

    def nine(pad, n, dst, row):
        rows = pad.shape[0]
        for kh in range(3):
            for kw in range(3):
                begin = PAD + n * size + (kh - 1) * W + kw - 1
                value = pad[:, begin:begin + size]
                if kw == 0:
                    value = value * left
                elif kw == 2:
                    value = value * right
                dst[row:row + rows, :] = value
                row += rows

    def halo_wait(n):
        @pl.when(has_down)
        def _():
            halo_up(n).wait_recv()

        @pl.when(has_up)
        def _():
            halo_down(n).wait_recv()

    def step1(n):
        return remote(s1s.at[n], s1r.at[n], s1_ss.at[n], s1_rs.at[n], {"chan": sibling})

    def first(n):
        if n == 0:
            halo_wait(0)
        if n + 1 < CHUNKS:
            halo_wait(n + 1)
        for kd, pad in enumerate((xlo, xmid, xhi)):
            nine(pad, n, cols1, kd * 9 * chan)
        acc = jnp.dot(w1t[...], cols1[...], preferred_element_type=jnp.float32)
        for j in range(half):
            even = acc[2 * j * chan:(2 * j + 1) * chan]
            odd = acc[(2 * j + 1) * chan:(2 * j + 2) * chan]
            rows = slice(j * chan, (j + 1) * chan)
            keep[n, rows, :] = jnp.where(core == 0, even, odd)
            s1s[n, rows, :] = jnp.where(core == 0, odd, even).astype(jnp.bfloat16)
        step1(n).start()

    def step2(n, k):
        block = pl.ds(pl.multiple_of(lax.rem(chip + k, half) * chan, chan), chan)
        return remote(s2s.at[n, block], s2r.at[n, k - 1], s2_ss.at[n, k - 1], s2_rs.at[n, k - 1],
                      {"chan": peer(k)})

    def second(n):
        step1(n).wait_recv()
        both = keep[n] + s1r[n].astype(jnp.float32)
        keep[n] = both
        s2s[n] = both.astype(jnp.bfloat16)
        for k in range(1, half):
            step2(n, k).start()

    def block_of(owner, n):
        return hpad.at[pl.ds(pl.multiple_of(owner * chan, chan), chan), pl.ds(PAD + n * size, size)]

    def gather_peer(n, k):
        here = block_of(c, n)
        return remote(here, here, ag_ss.at[n, k], ag_rs.at[n, k], {"chan": peer(k)})

    def gather_sibling(n, k):
        here = block_of(peer(half - k), n)
        return remote(here, here, ag_ss.at[n, half + k], ag_rs.at[n, half + k], {"chan": sibling})

    def third(n):
        total_sum = keep[n, pl.ds(pl.multiple_of(chip * chan, chan), chan), :]
        for k in range(1, half):
            step2(n, k).wait_recv()
            total_sum = total_sum + s2r[n, k - 1].astype(jnp.float32)
        hidden = jnp.maximum(total_sum + b1[...], 0.0).astype(jnp.bfloat16)
        hpad[pl.ds(pl.multiple_of(c * chan, chan), chan), PAD + n * size:PAD + (n + 1) * size] = hidden
        for k in range(1, half):
            gather_peer(n, k).start()
        gather_sibling(n, 0).start()

    def forward(n):
        for k in range(1, half):
            gather_peer(n, k).wait_recv()
            gather_sibling(n, k).start()

    def gathered(n):
        for k in range(half):
            gather_sibling(n, k).wait_recv()

    def partial_up(n):
        columns = pl.ds(n * size, size)
        return remote(ps.at[0, :, columns], pr.at[0, :, columns], par_s.at[0, n], par_r.at[0, n],
                      {"depth": d + 1})

    def partial_down(n):
        columns = pl.ds(n * size, size)
        return remote(ps.at[1, :, columns], pr.at[1, :, columns], par_s.at[1, n], par_r.at[1, n],
                      {"depth": d - 1})

    def fourth(n):
        nine(hpad, n, cols2, 0)
        acc = jnp.dot(w2t[...], cols2[...], preferred_element_type=jnp.float32)
        columns = slice(n * size, (n + 1) * size)
        ps[0, :, columns] = acc[0:chan].astype(jnp.bfloat16)
        ps[1, :, columns] = acc[2 * chan:3 * chan].astype(jnp.bfloat16)

        @pl.when(has_up)
        def _():
            partial_up(n).start()

        @pl.when(has_down)
        def _():
            partial_down(n).start()

        keep2[:, columns] = acc[chan:2 * chan] + b2[...]

    def last(n):
        @pl.when(has_down)
        def _():
            partial_up(n).wait_recv()

        @pl.when(has_up)
        def _():
            partial_down(n).wait_recv()

        columns = slice(n * size, (n + 1) * size)
        value = keep2[:, columns] + pr[0, :, columns].astype(jnp.float32)
        out[:, columns] = (value + pr[1, :, columns].astype(jnp.float32)).astype(jnp.bfloat16)

    for t in range(CHUNKS + 4):
        if t < CHUNKS:
            first(t)
            second(t)
        if 0 <= t - 1 < CHUNKS:
            third(t - 1)
            forward(t - 1)
        if 0 <= t - 2 < CHUNKS:
            gathered(t - 2)
        if 0 <= t - 3 < CHUNKS:
            fourth(t - 3)
    for n in range(CHUNKS):
        last(n)

    for n in range(CHUNKS):
        @pl.when(has_up)
        def _():
            halo_up(n).wait_send()
            partial_up(n).wait_send()

        @pl.when(has_down)
        def _():
            halo_down(n).wait_send()
            partial_down(n).wait_send()

        step1(n).wait_send()
        gather_sibling(n, 0).wait_send()
        for k in range(1, half):
            step2(n, k).wait_send()
            gather_peer(n, k).wait_send()
            gather_sibling(n, k).wait_send()


def body(nd, nc, volume, w_first, b_first, w_second, b_second):
    chan, slab, cells = volume.shape
    total, half, size = chan * nc, nc // 2, cells // CHUNKS
    bf16, f32 = jnp.bfloat16, jnp.float32
    vmem = pl.BlockSpec(memory_space=pltpu.VMEM)
    dma = pltpu.SemaphoreType.DMA
    wide = cells + 2 * PAD
    out = pl.pallas_call(
        functools.partial(kernel, nd, nc),
        out_shape=jax.ShapeDtypeStruct((chan, cells), bf16),
        in_specs=[vmem] * 5,
        out_specs=vmem,
        scratch_shapes=[
            pltpu.VMEM((chan, wide), bf16),
            pltpu.VMEM((chan, wide), bf16),
            pltpu.VMEM((chan, wide), bf16),
            pltpu.VMEM((total, 27 * chan), bf16),
            pltpu.VMEM((3 * chan, 9 * total), bf16),
            pltpu.VMEM((27 * chan, size), bf16),
            pltpu.VMEM((9 * total, size), bf16),
            pltpu.VMEM((CHUNKS, half * chan, size), bf16),
            pltpu.VMEM((CHUNKS, half * chan, size), bf16),
            pltpu.VMEM((CHUNKS, half * chan, size), f32),
            pltpu.VMEM((CHUNKS, half * chan, size), bf16),
            pltpu.VMEM((CHUNKS, half - 1, chan, size), bf16),
            pltpu.VMEM((total, wide), bf16),
            pltpu.VMEM((2, chan, cells), bf16),
            pltpu.VMEM((2, chan, cells), bf16),
            pltpu.VMEM((chan, cells), f32),
            dma((2, CHUNKS)), dma((2, CHUNKS)),
            dma((CHUNKS,)), dma((CHUNKS,)),
            dma((CHUNKS, half - 1)), dma((CHUNKS, half - 1)),
            dma((CHUNKS, 2 * half)), dma((CHUNKS, 2 * half)),
            dma((2, CHUNKS)), dma((2, CHUNKS)),
        ],
        compiler_params=pltpu.CompilerParams(
            collective_id=0, has_side_effects=True, vmem_limit_bytes=56 * 1024 * 1024),
    )(
        volume.reshape(chan, cells),
        w_first.reshape(27 * chan, total),
        b_first.reshape(chan, 1),
        w_second,
        b_second.reshape(chan, 1),
    )
    return out.reshape(chan, slab, cells)


def solution(mesh):
    in_specs = (
        P("chan", "depth", None),
        P(None, "chan", None),
        P("chan"),
        P(None, None, "chan"),
        P("chan"),
    )
    out_specs = P("chan", "depth", None)
    inner = functools.partial(body, mesh.shape["depth"], mesh.shape["chan"])
    return jax.shard_map(inner, mesh=mesh, in_specs=in_specs, out_specs=out_specs, check_vma=False)
```

```python
import functools

import jax
import jax.numpy as jnp
from jax import lax
from jax.experimental import pallas as pl
from jax.experimental.pallas import tpu as pltpu
from jax.sharding import PartitionSpec as P

W = 64
PAD = 128
MESH = pl.DeviceIdType.MESH


def kernel(nd, nc, vol, w1, b1, w2, b2, out,
           xs, w1t, w2t, cols1, cols2, s1s, s1r, keep, s2s, s2r,
           hpad, ps, pr, total_a, total_b, done, landed,
           pair_s, pair_r, z_s, z_r, s1_ss, s1_rs, s2_ss, s2_rs, ag_ss, ag_rs, par_s, par_r):
    chan, cells = vol.shape
    total = chan * nc
    half = nc // 2
    inner = cells // 2
    seg = inner + PAD
    skip = inner - PAD
    spans, spans2, pieces = chunk_spans(cells)
    count = len(spans)
    d = lax.axis_index("depth")
    c = lax.axis_index("chan")
    side = lax.rem(d, 2)
    partner = d + 1 - 2 * side
    core = lax.rem(c, 2)
    chip = c // 2
    sibling = 2 * chip + 1 - core
    has_up = d + 2 < nd
    has_down = d >= 2

    def peer(k):
        return 2 * lax.rem(chip + k, half) + core

    for plane in range(4):
        xs[plane, :, 0:PAD] = jnp.zeros((chan, PAD), jnp.bfloat16)
        xs[plane, :, PAD + seg:] = jnp.zeros((chan, PAD), jnp.bfloat16)
    for plane in range(2):
        hpad[plane, :, 0:PAD] = jnp.zeros((total, PAD), jnp.bfloat16)
        hpad[plane, :, PAD + seg:] = jnp.zeros((total, PAD), jnp.bfloat16)

    @pl.when(jnp.logical_not(has_down))
    def _():
        xs[0, :, PAD:PAD + seg] = jnp.zeros((chan, seg), jnp.bfloat16)
        pr[0] = jnp.zeros((chan, seg), jnp.bfloat16)

    @pl.when(jnp.logical_not(has_up))
    def _():
        xs[3, :, PAD:PAD + seg] = jnp.zeros((chan, seg), jnp.bfloat16)
        pr[1] = jnp.zeros((chan, seg), jnp.bfloat16)

    barrier = pltpu.get_barrier_semaphore()

    @pl.when(has_up)
    def _():
        pl.semaphore_signal(barrier, inc=1, device_id={"depth": d + 2}, device_id_type=MESH)

    @pl.when(has_down)
    def _():
        pl.semaphore_signal(barrier, inc=1, device_id={"depth": d - 2}, device_id_type=MESH)

    pl.semaphore_signal(barrier, inc=1, device_id={"depth": partner}, device_id_type=MESH)
    pl.semaphore_signal(barrier, inc=1, device_id={"chan": sibling}, device_id_type=MESH)
    for k in range(1, half):
        pl.semaphore_signal(barrier, inc=1, device_id={"chan": peer(k)}, device_id_type=MESH)
    pl.semaphore_wait(barrier, half + 1 + has_up.astype(jnp.int32) + has_down.astype(jnp.int32))

    def remote(src, dst, send, recv, where):
        return pltpu.make_async_remote_copy(
            src_ref=src, dst_ref=dst, send_sem=send, recv_sem=recv,
            device_id=where, device_id_type=MESH)

    def swap(i):
        start, size = pieces[i]
        theirs = pl.ds(pl.multiple_of((1 - side) * skip + start, PAD), size)
        return remote(vol.at[:, theirs], xs.at[1 + side, :, pl.ds(PAD + start, size)],
                      pair_s.at[i], pair_r.at[i], {"depth": partner})

    def send_up(i):
        data = pl.ds(PAD + pieces[i][0], pieces[i][1])
        return remote(xs.at[2, :, data], xs.at[0, :, data], z_s.at[0, i], z_r.at[0, i], {"depth": d + 2})

    def send_down(i):
        data = pl.ds(PAD + pieces[i][0], pieces[i][1])
        return remote(xs.at[1, :, data], xs.at[3, :, data], z_s.at[1, i], z_r.at[1, i], {"depth": d - 2})

    def own_out(i):
        @pl.when(jnp.logical_and(side == 0, has_down))
        def _():
            send_down(i).start()

        @pl.when(jnp.logical_and(side == 1, has_up))
        def _():
            send_up(i).start()

    def relay(i):
        swap(i).wait_recv()

        @pl.when(jnp.logical_and(side == 1, has_down))
        def _():
            send_down(i).start()

        @pl.when(jnp.logical_and(side == 0, has_up))
        def _():
            send_up(i).start()

    swap(0).start()
    xs[1 + side, :, PAD:PAD + seg] = vol[:, pl.ds(pl.multiple_of(side * skip, PAD), seg)]
    own_out(0)
    bias1 = jnp.broadcast_to(b1[...], (8, chan)).T[:, 0:1]
    bias2 = jnp.broadcast_to(b2[...], (8, chan)).T[:, 0:1]
    taps = 27 * chan
    for begin in range(0, taps, 128):
        end = min(begin + 128, taps)
        w1t[:, begin:end] = w1[begin:end, :].T
    relay(0)
    swap(1).start()
    own_out(1)
    for kd in range(3):
        for kk in range(9):
            w2t[kd * chan:(kd + 1) * chan, kk * total:(kk + 1) * total] = w2[kd * 9 + kk]

    def nine(pad, plane, start, size, dst, row):
        rows = pad.shape[1]
        column = lax.broadcasted_iota(jnp.int32, (1, size), 1) % W
        left = jnp.where(column >= 1, 1.0, 0.0).astype(jnp.bfloat16)
        right = jnp.where(column < W - 1, 1.0, 0.0).astype(jnp.bfloat16)
        for kh in range(3):
            for kw in range(3):
                begin = PAD + start + (kh - 1) * W + kw - 1
                value = pad[plane, :, begin:begin + size]
                if kw == 0:
                    value = value * left
                elif kw == 2:
                    value = value * right
                dst[row:row + rows, 0:size] = value
                row += rows

    def step1(n):
        size = spans[n][2]
        return remote(s1s.at[n, :, pl.ds(0, size)], s1r.at[n, :, pl.ds(0, size)],
                      s1_ss.at[n], s1_rs.at[n], {"chan": sibling})

    def first(n):
        plane, start, size = spans[n]
        for kd in range(3):
            nine(xs, plane + kd, start, size, cols1, kd * 9 * chan)
        acc = jnp.dot(w1t[...], cols1[:, 0:size], preferred_element_type=jnp.float32)
        for j in range(half):
            even = acc[2 * j * chan:(2 * j + 1) * chan]
            odd = acc[(2 * j + 1) * chan:(2 * j + 2) * chan]
            rows = slice(j * chan, (j + 1) * chan)
            keep[n, rows, 0:size] = jnp.where(core == 0, even, odd)
            s1s[n, rows, 0:size] = jnp.where(core == 0, odd, even).astype(jnp.bfloat16)
        step1(n).start()

    def step2(n, k):
        size = spans[n][2]
        block = pl.ds(pl.multiple_of(lax.rem(chip + k, half) * chan, chan), chan)
        return remote(s2s.at[n, block, pl.ds(0, size)], s2r.at[n, k - 1, :, pl.ds(0, size)],
                      s2_ss.at[n, k - 1], s2_rs.at[n, k - 1], {"chan": peer(k)})

    def second(n):
        size = spans[n][2]
        step1(n).wait_recv()
        both = keep[n, :, 0:size] + s1r[n, :, 0:size].astype(jnp.float32)
        keep[n, :, 0:size] = both
        s2s[n, :, 0:size] = both.astype(jnp.bfloat16)
        for k in range(1, half):
            step2(n, k).start()

    def block_of(owner, n):
        plane, start, size = spans[n]
        return hpad.at[plane, pl.ds(pl.multiple_of(owner * chan, chan), chan), pl.ds(PAD + start, size)]

    def gather_peer(n, k):
        here = block_of(c, n)
        return remote(here, here, ag_ss.at[n, k], ag_rs.at[n, k], {"chan": peer(k)})

    def gather_sibling(n, k):
        here = block_of(peer(half - k), n)
        return remote(here, here, ag_ss.at[n, half + k], ag_rs.at[n, half + k], {"chan": sibling})

    def third(n):
        plane, start, size = spans[n]
        value = keep[n, pl.ds(pl.multiple_of(chip * chan, chan), chan), 0:size]
        for k in range(1, half):
            step2(n, k).wait_recv()
            value = value + s2r[n, k - 1, :, 0:size].astype(jnp.float32)
        hidden = jnp.maximum(value + bias1, 0.0).astype(jnp.bfloat16)
        hpad[plane, pl.ds(pl.multiple_of(c * chan, chan), chan), PAD + start:PAD + start + size] = hidden
        for k in range(1, half):
            gather_peer(n, k).start()
        gather_sibling(n, 0).start()

    def forward(n):
        for k in range(1, half):
            gather_peer(n, k).wait_recv()
            gather_sibling(n, k).start()

    def gathered(n):
        for k in range(half):
            gather_sibling(n, k).wait_recv()

    def partial(n):
        plane, start, size = spans2[n]
        columns = pl.ds(start, size)
        index = 1 - plane
        return remote(ps.at[index, :, columns], pr.at[index, :, columns],
                      par_s.at[n], par_r.at[n], {"depth": d + 4 * plane - 2})

    def fourth(n):
        plane, start, size = spans2[n]
        nine(hpad, plane, start, size, cols2, 0)
        acc = jnp.dot(w2t[...], cols2[:, 0:size], preferred_element_type=jnp.float32)
        columns = slice(start, start + size)
        below, same, above = acc[0:chan], acc[chan:2 * chan], acc[2 * chan:3 * chan]
        if plane == 0:
            ps[1, :, columns] = above.astype(jnp.bfloat16)
            total_a[:, columns] = same + bias2
            total_b[:, columns] = below + bias2
        else:
            ps[0, :, columns] = below.astype(jnp.bfloat16)
            total_a[:, columns] = total_a[:, columns] + above
            total_b[:, columns] = total_b[:, columns] + same

        @pl.when(has_up if plane else has_down)
        def _():
            partial(n).start()

    def last(n):
        plane, start, size = spans2[n]

        @pl.when(has_down if plane else has_up)
        def _():
            partial(n).wait_recv()

        columns = slice(start, start + size)
        index = 1 - plane
        held = total_b if index else total_a
        value = held[:, columns] + pr[index, :, columns].astype(jnp.float32)
        done[index, :, columns] = value.astype(jnp.bfloat16)

    def arrived(t):
        @pl.when(has_up if t % 2 else has_down)
        def _():
            (send_down if t % 2 else send_up)(t // 2).wait_recv()

    tail = inner // 2 + PAD
    parts = [(0, inner - tail), (inner - tail, tail)]

    def back(i):
        start, size = parts[i]
        return remote(done.at[1 - side, :, pl.ds(pl.multiple_of(side * PAD + start, PAD), size)],
                      landed.at[:, pl.ds(start, size)], pair_s.at[2 + i], pair_r.at[2 + i],
                      {"depth": partner})

    def finish(i):
        last(2 * i)
        last(2 * i + 1)
        back(i).start()

    for t in range(count + 2):
        if t < count:
            arrived(t)
            first(t)
            if t == 0:
                relay(1)
        if 0 <= t - 1 < count:
            third(t - 1)
        if t < count:
            second(t)
        if 0 <= t - 2 < count:
            gathered(t - 2)
            fourth(t - 2)
        if 0 <= t - 1 < count:
            forward(t - 1)
        if t == count:
            finish(0)
    finish(1)

    out[:, pl.ds(pl.multiple_of(side * inner, PAD), inner)] = done[
        side, :, pl.ds(pl.multiple_of(side * PAD, PAD), inner)]
    for i, (start, size) in enumerate(parts):
        back(i).wait_recv()
        out[:, pl.ds(pl.multiple_of((1 - side) * inner + start, PAD), size)] = landed[:, start:start + size]

    for i in range(2):
        back(i).wait_send()
        swap(i).wait_send()

        @pl.when(has_up)
        def _():
            send_up(i).wait_send()

        @pl.when(has_down)
        def _():
            send_down(i).wait_send()

    for n in range(count):
        @pl.when(has_up if spans[n][0] else has_down)
        def _():
            partial(n).wait_send()

        step1(n).wait_send()
        gather_sibling(n, 0).wait_send()
        for k in range(1, half):
            step2(n, k).wait_send()
            gather_peer(n, k).wait_send()
            gather_sibling(n, k).wait_send()


def chunk_spans(cells):
    seg = cells // 2 + PAD
    cut = (seg // 2 + PAD - 1) // PAD * PAD
    early = cut - PAD
    first = [(plane, start, size) for start, size in ((0, cut), (cut, seg - cut)) for plane in range(2)]
    second = [(plane, start, size) for start, size in ((0, early), (early, seg - early)) for plane in range(2)]
    pieces = [(0, cut + PAD), (cut + PAD, seg - cut - PAD)]
    return first, second, pieces


def body(nd, nc, volume, w_first, b_first, w_second, b_second):
    chan, slab, cells = volume.shape
    total, half = chan * nc, nc // 2
    spans, spans2, pieces = chunk_spans(cells)
    count = len(spans)
    size = max(span[2] for span in spans + spans2)
    seg = cells // 2 + PAD
    bf16, f32 = jnp.bfloat16, jnp.float32
    vmem = pl.BlockSpec(memory_space=pltpu.VMEM)
    dma = pltpu.SemaphoreType.DMA
    wide = seg + 2 * PAD
    out = pl.pallas_call(
        functools.partial(kernel, nd, nc),
        out_shape=jax.ShapeDtypeStruct((chan, cells), bf16),
        in_specs=[vmem] * 5,
        out_specs=vmem,
        scratch_shapes=[
            pltpu.VMEM((4, chan, wide), bf16),
            pltpu.VMEM((total, 27 * chan), bf16),
            pltpu.VMEM((3 * chan, 9 * total), bf16),
            pltpu.VMEM((27 * chan, size), bf16),
            pltpu.VMEM((9 * total, size), bf16),
            pltpu.VMEM((count, half * chan, size), bf16),
            pltpu.VMEM((count, half * chan, size), bf16),
            pltpu.VMEM((count, half * chan, size), f32),
            pltpu.VMEM((count, half * chan, size), bf16),
            pltpu.VMEM((count, half - 1, chan, size), bf16),
            pltpu.VMEM((2, total, wide), bf16),
            pltpu.VMEM((2, chan, seg), bf16),
            pltpu.VMEM((2, chan, seg), bf16),
            pltpu.VMEM((chan, seg), f32),
            pltpu.VMEM((chan, seg), f32),
            pltpu.VMEM((2, chan, seg), bf16),
            pltpu.VMEM((chan, cells // 2), bf16),
            dma((4,)), dma((4,)), dma((2, 2)), dma((2, 2)),
            dma((count,)), dma((count,)),
            dma((count, half - 1)), dma((count, half - 1)),
            dma((count, 2 * half)), dma((count, 2 * half)),
            dma((count,)), dma((count,)),
        ],
        compiler_params=pltpu.CompilerParams(
            collective_id=0, has_side_effects=True, vmem_limit_bytes=56 * 1024 * 1024),
    )(
        volume.reshape(chan, cells),
        w_first.reshape(27 * chan, total),
        b_first.reshape(1, chan),
        jnp.swapaxes(w_second, 1, 2),
        b_second.reshape(1, chan),
    )
    return out.reshape(chan, slab, cells)


def solution(mesh):
    in_specs = (
        P("chan", "depth", None),
        P(None, "chan", None),
        P("chan"),
        P(None, None, "chan"),
        P("chan"),
    )
    out_specs = P("chan", "depth", None)
    inner = functools.partial(body, mesh.shape["depth"], mesh.shape["chan"])
    return jax.shard_map(inner, mesh=mesh, in_specs=in_specs, out_specs=out_specs, check_vma=False)
```

```python
import functools

import jax
import jax.numpy as jnp
from jax import lax
from jax.experimental import pallas as pl
from jax.experimental.pallas import tpu as pltpu
from jax.sharding import PartitionSpec as P

W = 64
PAD = 128
MESH = pl.DeviceIdType.MESH


def kernel(nd, nc, vol, w1, b1, w2, b2, out,
           xs, w1t, w2t, cols1, cols2, s1s, s1r, keep, s2s, s2r,
           hpad, ps, pr, total_a, total_b, done, landed,
           pair_s, pair_r, z_s, z_r, s1_ss, s1_rs, s2_ss, s2_rs, ag_ss, ag_rs, par_s, par_r):
    chan, cells = vol.shape
    total = chan * nc
    half = nc // 2
    inner = cells // 2
    seg = inner + PAD
    skip = inner - PAD
    spans, spans2, pieces = chunk_spans(cells)
    count = len(spans)
    d = lax.axis_index("depth")
    c = lax.axis_index("chan")
    side = lax.rem(d, 2)
    partner = d + 1 - 2 * side
    core = lax.rem(c, 2)
    chip = c // 2
    sibling = 2 * chip + 1 - core
    has_up = d + 2 < nd
    has_down = d >= 2

    def peer(k):
        return 2 * lax.rem(chip + k, half) + core

    for plane in range(4):
        xs[plane, :, 0:PAD] = jnp.zeros((chan, PAD), jnp.bfloat16)
        xs[plane, :, PAD + seg:] = jnp.zeros((chan, PAD), jnp.bfloat16)
    for plane in range(2):
        hpad[plane, :, 0:PAD] = jnp.zeros((total, PAD), jnp.bfloat16)
        hpad[plane, :, PAD + seg:] = jnp.zeros((total, PAD), jnp.bfloat16)

    @pl.when(jnp.logical_not(has_down))
    def _():
        xs[0, :, PAD:PAD + seg] = jnp.zeros((chan, seg), jnp.bfloat16)
        pr[0] = jnp.zeros((chan, seg), jnp.bfloat16)

    @pl.when(jnp.logical_not(has_up))
    def _():
        xs[3, :, PAD:PAD + seg] = jnp.zeros((chan, seg), jnp.bfloat16)
        pr[1] = jnp.zeros((chan, seg), jnp.bfloat16)

    barrier = pltpu.get_barrier_semaphore()

    @pl.when(has_up)
    def _():
        pl.semaphore_signal(barrier, inc=1, device_id={"depth": d + 2}, device_id_type=MESH)

    @pl.when(has_down)
    def _():
        pl.semaphore_signal(barrier, inc=1, device_id={"depth": d - 2}, device_id_type=MESH)

    pl.semaphore_signal(barrier, inc=1, device_id={"depth": partner}, device_id_type=MESH)
    pl.semaphore_signal(barrier, inc=1, device_id={"chan": sibling}, device_id_type=MESH)
    for k in range(1, half):
        pl.semaphore_signal(barrier, inc=1, device_id={"chan": peer(k)}, device_id_type=MESH)
    pl.semaphore_wait(barrier, half + 1 + has_up.astype(jnp.int32) + has_down.astype(jnp.int32))

    def remote(src, dst, send, recv, where):
        return pltpu.make_async_remote_copy(
            src_ref=src, dst_ref=dst, send_sem=send, recv_sem=recv,
            device_id=where, device_id_type=MESH)

    def swap(i):
        start, size = pieces[i]
        theirs = pl.ds(pl.multiple_of((1 - side) * skip + start, PAD), size)
        return remote(vol.at[:, theirs], xs.at[1 + side, :, pl.ds(PAD + start, size)],
                      pair_s.at[i], pair_r.at[i], {"depth": partner})

    def send_up(i):
        data = pl.ds(PAD + pieces[i][0], pieces[i][1])
        return remote(xs.at[2, :, data], xs.at[0, :, data], z_s.at[0, i], z_r.at[0, i], {"depth": d + 2})

    def send_down(i):
        data = pl.ds(PAD + pieces[i][0], pieces[i][1])
        return remote(xs.at[1, :, data], xs.at[3, :, data], z_s.at[1, i], z_r.at[1, i], {"depth": d - 2})

    def own_out(i):
        @pl.when(jnp.logical_and(side == 0, has_down))
        def _():
            send_down(i).start()

        @pl.when(jnp.logical_and(side == 1, has_up))
        def _():
            send_up(i).start()

    def relay(i):
        swap(i).wait_recv()

        @pl.when(jnp.logical_and(side == 1, has_down))
        def _():
            send_down(i).start()

        @pl.when(jnp.logical_and(side == 0, has_up))
        def _():
            send_up(i).start()

    swap(0).start()
    xs[1 + side, :, PAD:PAD + seg] = vol[:, pl.ds(pl.multiple_of(side * skip, PAD), seg)]
    own_out(0)
    bias1 = jnp.broadcast_to(b1[...], (8, chan)).T[:, 0:1]
    bias2 = jnp.broadcast_to(b2[...], (8, chan)).T[:, 0:1]
    taps = 27 * chan
    for begin in range(0, taps, 128):
        end = min(begin + 128, taps)
        w1t[:, begin:end] = w1[begin:end, :].T
    relay(0)
    swap(1).start()
    own_out(1)
    for kd in range(3):
        for kk in range(9):
            w2t[kd * chan:(kd + 1) * chan, kk * total:(kk + 1) * total] = w2[kd * 9 + kk]

    def nine(pad, plane, start, size, dst, row):
        rows = pad.shape[1]
        column = lax.broadcasted_iota(jnp.int32, (1, size), 1) % W
        left = jnp.where(column >= 1, 1.0, 0.0).astype(jnp.bfloat16)
        right = jnp.where(column < W - 1, 1.0, 0.0).astype(jnp.bfloat16)
        for kh in range(3):
            for kw in range(3):
                begin = PAD + start + (kh - 1) * W + kw - 1
                value = pad[plane, :, begin:begin + size]
                if kw == 0:
                    value = value * left
                elif kw == 2:
                    value = value * right
                dst[row:row + rows, 0:size] = value
                row += rows

    def step1(n):
        size = spans[n][2]
        return remote(s1s.at[n, :, pl.ds(0, size)], s1r.at[n, :, pl.ds(0, size)],
                      s1_ss.at[n], s1_rs.at[n], {"chan": sibling})

    def first(n):
        plane, start, size = spans[n]
        for kd in range(3):
            nine(xs, plane + kd, start, size, cols1, kd * 9 * chan)
        acc = jnp.dot(w1t[...], cols1[:, 0:size], preferred_element_type=jnp.float32)
        for j in range(half):
            even = acc[2 * j * chan:(2 * j + 1) * chan]
            odd = acc[(2 * j + 1) * chan:(2 * j + 2) * chan]
            rows = slice(j * chan, (j + 1) * chan)
            keep[n, rows, 0:size] = jnp.where(core == 0, even, odd)
            s1s[n, rows, 0:size] = jnp.where(core == 0, odd, even).astype(jnp.bfloat16)
        step1(n).start()

    def step2(n, k):
        size = spans[n][2]
        block = pl.ds(pl.multiple_of(lax.rem(chip + k, half) * chan, chan), chan)
        return remote(s2s.at[n, block, pl.ds(0, size)], s2r.at[n, k - 1, :, pl.ds(0, size)],
                      s2_ss.at[n, k - 1], s2_rs.at[n, k - 1], {"chan": peer(k)})

    def second(n):
        size = spans[n][2]
        step1(n).wait_recv()
        both = keep[n, :, 0:size] + s1r[n, :, 0:size].astype(jnp.float32)
        keep[n, :, 0:size] = both
        s2s[n, :, 0:size] = both.astype(jnp.bfloat16)
        for k in range(1, half):
            step2(n, k).start()

    def block_of(owner, n):
        plane, start, size = spans[n]
        return hpad.at[plane, pl.ds(pl.multiple_of(owner * chan, chan), chan), pl.ds(PAD + start, size)]

    def gather_peer(n, k):
        here = block_of(c, n)
        return remote(here, here, ag_ss.at[n, k], ag_rs.at[n, k], {"chan": peer(k)})

    def gather_sibling(n, k):
        here = block_of(peer(half - k), n)
        return remote(here, here, ag_ss.at[n, half + k], ag_rs.at[n, half + k], {"chan": sibling})

    def third(n):
        plane, start, size = spans[n]
        value = keep[n, pl.ds(pl.multiple_of(chip * chan, chan), chan), 0:size]
        for k in range(1, half):
            step2(n, k).wait_recv()
            value = value + s2r[n, k - 1, :, 0:size].astype(jnp.float32)
        hidden = jnp.maximum(value + bias1, 0.0).astype(jnp.bfloat16)
        hpad[plane, pl.ds(pl.multiple_of(c * chan, chan), chan), PAD + start:PAD + start + size] = hidden
        for k in range(1, half):
            gather_peer(n, k).start()
        gather_sibling(n, 0).start()

    def forward(n):
        for k in range(1, half):
            gather_peer(n, k).wait_recv()
            gather_sibling(n, k).start()

    def gathered(n):
        for k in range(half):
            gather_sibling(n, k).wait_recv()

    def partial(n):
        plane, start, size = spans2[n]
        columns = pl.ds(start, size)
        index = 1 - plane
        return remote(ps.at[index, :, columns], pr.at[index, :, columns],
                      par_s.at[n], par_r.at[n], {"depth": d + 4 * plane - 2})

    def fourth(n):
        plane, start, size = spans2[n]
        nine(hpad, plane, start, size, cols2, 0)
        acc = jnp.dot(w2t[...], cols2[:, 0:size], preferred_element_type=jnp.float32)
        columns = slice(start, start + size)
        below, same, above = acc[0:chan], acc[chan:2 * chan], acc[2 * chan:3 * chan]
        if plane == 0:
            ps[1, :, columns] = above.astype(jnp.bfloat16)
            total_a[:, columns] = same + bias2
            total_b[:, columns] = below + bias2
        else:
            ps[0, :, columns] = below.astype(jnp.bfloat16)
            total_a[:, columns] = total_a[:, columns] + above
            total_b[:, columns] = total_b[:, columns] + same

        @pl.when(has_up if plane else has_down)
        def _():
            partial(n).start()

    def last(n):
        plane, start, size = spans2[n]

        @pl.when(has_down if plane else has_up)
        def _():
            partial(n).wait_recv()

        columns = slice(start, start + size)
        index = 1 - plane
        held = total_b if index else total_a
        value = held[:, columns] + pr[index, :, columns].astype(jnp.float32)
        done[index, :, columns] = value.astype(jnp.bfloat16)

    def arrived(t):
        @pl.when(has_up if t % 2 else has_down)
        def _():
            (send_down if t % 2 else send_up)(t // 2).wait_recv()

    tail = inner // 2 + PAD
    parts = [(0, inner - tail), (inner - tail, tail)]

    def back(i):
        start, size = parts[i]
        return remote(done.at[1 - side, :, pl.ds(pl.multiple_of(side * PAD + start, PAD), size)],
                      landed.at[:, pl.ds(start, size)], pair_s.at[2 + i], pair_r.at[2 + i],
                      {"depth": partner})

    def finish(i):
        last(2 * i)
        last(2 * i + 1)
        back(i).start()

    for t in range(count + 2):
        if t < count:
            arrived(t)
            first(t)
            if t == 0:
                relay(1)
        if 0 <= t - 1 < count:
            third(t - 1)
        if 0 <= t - 2 < count:
            gathered(t - 2)
            fourth(t - 2)
        if t < count:
            second(t)
        if 0 <= t - 1 < count:
            forward(t - 1)
        if t == count:
            finish(0)
    finish(1)

    out[:, pl.ds(pl.multiple_of(side * inner, PAD), inner)] = done[
        side, :, pl.ds(pl.multiple_of(side * PAD, PAD), inner)]
    for i, (start, size) in enumerate(parts):
        back(i).wait_recv()
        out[:, pl.ds(pl.multiple_of((1 - side) * inner + start, PAD), size)] = landed[:, start:start + size]

    for i in range(2):
        back(i).wait_send()
        swap(i).wait_send()

        @pl.when(has_up)
        def _():
            send_up(i).wait_send()

        @pl.when(has_down)
        def _():
            send_down(i).wait_send()

    for n in range(count):
        @pl.when(has_up if spans[n][0] else has_down)
        def _():
            partial(n).wait_send()

        step1(n).wait_send()
        gather_sibling(n, 0).wait_send()
        for k in range(1, half):
            step2(n, k).wait_send()
            gather_peer(n, k).wait_send()
            gather_sibling(n, k).wait_send()


def chunk_spans(cells):
    seg = cells // 2 + PAD
    cut = (seg // 2 + PAD - 1) // PAD * PAD
    early = cut - PAD
    first = [(plane, start, size) for start, size in ((0, cut), (cut, seg - cut)) for plane in range(2)]
    second = [(plane, start, size) for start, size in ((0, early), (early, seg - early)) for plane in range(2)]
    pieces = [(0, cut + PAD), (cut + PAD, seg - cut - PAD)]
    return first, second, pieces


def body(nd, nc, volume, w_first, b_first, w_second, b_second):
    chan, slab, cells = volume.shape
    total, half = chan * nc, nc // 2
    spans, spans2, pieces = chunk_spans(cells)
    count = len(spans)
    size = max(span[2] for span in spans + spans2)
    seg = cells // 2 + PAD
    bf16, f32 = jnp.bfloat16, jnp.float32
    vmem = pl.BlockSpec(memory_space=pltpu.VMEM)
    dma = pltpu.SemaphoreType.DMA
    wide = seg + 2 * PAD
    out = pl.pallas_call(
        functools.partial(kernel, nd, nc),
        out_shape=jax.ShapeDtypeStruct((chan, cells), bf16),
        in_specs=[vmem] * 5,
        out_specs=vmem,
        scratch_shapes=[
            pltpu.VMEM((4, chan, wide), bf16),
            pltpu.VMEM((total, 27 * chan), bf16),
            pltpu.VMEM((3 * chan, 9 * total), bf16),
            pltpu.VMEM((27 * chan, size), bf16),
            pltpu.VMEM((9 * total, size), bf16),
            pltpu.VMEM((count, half * chan, size), bf16),
            pltpu.VMEM((count, half * chan, size), bf16),
            pltpu.VMEM((count, half * chan, size), f32),
            pltpu.VMEM((count, half * chan, size), bf16),
            pltpu.VMEM((count, half - 1, chan, size), bf16),
            pltpu.VMEM((2, total, wide), bf16),
            pltpu.VMEM((2, chan, seg), bf16),
            pltpu.VMEM((2, chan, seg), bf16),
            pltpu.VMEM((chan, seg), f32),
            pltpu.VMEM((chan, seg), f32),
            pltpu.VMEM((2, chan, seg), bf16),
            pltpu.VMEM((chan, cells // 2), bf16),
            dma((4,)), dma((4,)), dma((2, 2)), dma((2, 2)),
            dma((count,)), dma((count,)),
            dma((count, half - 1)), dma((count, half - 1)),
            dma((count, 2 * half)), dma((count, 2 * half)),
            dma((count,)), dma((count,)),
        ],
        compiler_params=pltpu.CompilerParams(
            collective_id=0, has_side_effects=True, vmem_limit_bytes=56 * 1024 * 1024),
    )(
        volume.reshape(chan, cells),
        w_first.reshape(27 * chan, total),
        b_first.reshape(1, chan),
        jnp.swapaxes(w_second, 1, 2),
        b_second.reshape(1, chan),
    )
    return out.reshape(chan, slab, cells)


def solution(mesh):
    in_specs = (
        P("chan", "depth", None),
        P(None, "chan", None),
        P("chan"),
        P(None, None, "chan"),
        P("chan"),
    )
    out_specs = P("chan", "depth", None)
    inner = functools.partial(body, mesh.shape["depth"], mesh.shape["chan"])
    return jax.shard_map(inner, mesh=mesh, in_specs=in_specs, out_specs=out_specs, check_vma=False)
```
